256 devices in a mesh: view: 64 (over y, z, x_hi), head: 4 (over x_lo, core).
Axes of the slice: x: 4 (x_hi: 2, x_lo: 2; x = x_hi * 2 + x_lo), y: 4, z: 8, core: 2. Of those that a mesh axis runs over, the one named last changes fastest.
Arguments:
- queries: bfloat16 [256, 1280, 256], P('view', 'head'), may hold values from -6 to 6
- keys: bfloat16 [256, 1280, 256], P('view', 'head'), may hold values from -6 to 6
- values: bfloat16 [256, 1280, 256], P('view', 'head'), may hold values from -6 to 6
- out_grad: bfloat16 [256, 1280, 256], P('view', 'head'), may hold values from -6 to 6
- out_weight: bfloat16 [1280, 1280], P('head'), may hold values from -0.15625 to 0.15625
- visible: int32 [256, 7], P('view'), may hold values from 0 to 1, as said below
Outputs:
- query_grads: bfloat16 [256, 1280, 256], P('view', 'head')
- key_grads: bfloat16 [256, 1280, 256], P('view', 'head')
- value_grads: bfloat16 [256, 1280, 256], P('view', 'head')
The draws below stay inside these ranges and needn't reach their ends.
Inputs may be any that keep to these rules, and one draw needn't show every extreme that they name: `visible`: 1 wherever the offset's magnitude is 1 or 0; 0 or 1 elsewhere.
All inputs are finite; a program needn't handle non-finite values.
Results may differ from the reference program's by a relative error of at most 0.029.
Values may be sent and summed in bfloat16 or wider, within the bound.
No kernel may reach another device: no remote copies, remote signals or barrier semaphores. Data moves between devices by JAX's collectives and lax.ppermute only.
A program may use at most 128 MiB of HBM per device.

```python
import jax
import jax.numpy as jnp
from jax import lax

H = 20
DH = 64
R = 3
S = 256
D = 1280
VIEWS = 256


def draw_queries(key, part):
    key = jax.random.fold_in(key, 11)
    base = jnp.clip(jax.random.normal(key, (VIEWS, D, S), jnp.float32), -6.0, 6.0)
    return base.astype(jnp.bfloat16)


def draw_keys(key, part):
    key = jax.random.fold_in(key, 23)
    base = jnp.clip(jax.random.normal(key, (VIEWS, D, S), jnp.float32), -6.0, 6.0)
    return base.astype(jnp.bfloat16)


def draw_visible(key, part):
    key = jax.random.fold_in(key, 5)
    bits = jax.random.randint(key, (VIEWS, 2 * R + 1), 0, 2)
    offsets = jnp.arange(2 * R + 1) - R
    return jnp.where(jnp.abs(offsets)[None, :] <= 1, 1, bits).astype(jnp.int32)


def steps_of(rng, shape, shards, low, largest):
    loudness = 1.0
    for axis_at, shards_of in shards:
        steps = jax.random.uniform(jax.random.fold_in(jax.random.fold_in(rng, 6), axis_at), (shards_of,), jnp.float32, low / len(shards), largest / len(shards))
        loudness = loudness * jnp.repeat(jnp.exp(steps), shape[axis_at] // shards_of).reshape((-1,) + (1,) * (len(shape) - 1 - axis_at))
    return loudness


def gaussian(rng, dims, spread, bound, shards=(), held_as=jnp.bfloat16):
    factor_of = steps_of(rng, dims, shards, -0.22, 0.18) if shards else 1.0
    array = jax.random.normal(rng, dims, jnp.float32) * spread * factor_of
    return jnp.minimum(jnp.maximum(array, -bound), bound).astype(held_as)


def setup_inputs(seed: int = 0) -> dict:
    splits = jax.random.split(jax.random.key(seed), 7)
    queries = draw_queries(jax.random.fold_in(splits[6], 71), 0)
    keys = draw_keys(jax.random.fold_in(splits[6], 71), 0)
    values = gaussian(splits[2], (VIEWS, D, S), 1.0, 6.0, ((0, 64), (1, 4)))
    out_grad = gaussian(splits[3], (VIEWS, D, S), 1.0, 6.0, ((0, 64), (1, 4)))
    out_weight = gaussian(splits[4], (D, D), D ** -0.5, 0.15625, ((0, 4),))
    visible = draw_visible(jax.random.fold_in(splits[6], 71), 0)
    return {"queries": queries, "keys": keys, "values": values, "out_grad": out_grad, "out_weight": out_weight, "visible": visible}


def rounded(value):
    return lax.optimization_barrier(value.astype(jnp.bfloat16)).astype(jnp.float32)


def reference(queries, keys, values, out_grad, out_weight, visible):
    single = jnp.float32
    scale = DH ** -0.5
    views = queries.shape[0]
    span = 2 * R + 1
    attn_grad = rounded(jnp.einsum('ij,vjt->vit', out_weight.astype(single), out_grad.astype(single)))
    offsets = jnp.arange(span, dtype=jnp.int32) - R

    def one_view(carry, index):
        key_acc, value_acc = carry
        beside_all = ((index + offsets) % views).astype(jnp.int32)
        query_now = queries[index].astype(single).reshape(H, DH, -1)
        key_win = keys[beside_all].astype(single).reshape(span, H, DH, -1)
        value_win = values[beside_all].astype(single).reshape(span, H, DH, -1)
        grad_now = attn_grad[index].reshape(H, DH, -1)
        scores = jnp.einsum('hdt,ohdu->htou', query_now, key_win) * scale
        seen = visible[index] > 0
        scores = jnp.where(seen[None, None, :, None], scores, -jnp.inf)
        top = jnp.max(scores, axis=(2, 3), keepdims=True)
        total = jnp.sum(jnp.exp(scores - top), axis=(2, 3), keepdims=True)
        lse = top + jnp.log(total)
        probs = jnp.exp(scores - lse)
        probs_low = rounded(probs)
        output = rounded(jnp.einsum('htou,ohdu->hdt', probs_low, value_win))
        delta = jnp.sum(grad_now * output, axis=1)
        dprob = jnp.einsum('hdt,ohdu->htou', grad_now, value_win)
        dscore = rounded(probs * (dprob - delta[:, :, None, None]))
        query_grad = (scale * jnp.einsum('htou,ohdu->hdt', dscore, key_win)).astype(jnp.bfloat16)
        key_part = jnp.einsum('htou,hdt->ohdu', dscore, query_now).reshape(span, H * DH, -1)
        value_part = jnp.einsum('htou,hdt->ohdu', probs_low, grad_now).reshape(span, H * DH, -1)
        key_acc = key_acc.at[beside_all].add(key_part)
        value_acc = value_acc.at[beside_all].add(value_part)
        return (key_acc, value_acc), query_grad.reshape(H * DH, -1)

    zeros = jnp.zeros(queries.shape, single)
    (key_acc, value_acc), query_grads = lax.scan(one_view, (zeros, zeros), jnp.arange(views, dtype=jnp.int32))
    return query_grads, (scale * key_acc).astype(jnp.bfloat16), value_acc.astype(jnp.bfloat16)
```

```python
from functools import partial

import jax
import jax.numpy as jnp
from jax import lax
from jax.experimental import pallas as pl
from jax.experimental.pallas import tpu as pltpu
from jax.sharding import PartitionSpec as P

DH = 64
R = 3
CHUNKS = (2, 3)


def attn_kernel(vis_ref, q_ref, g_ref, k_ref, v_ref, hp_ref, hn_ref,
                dq_ref, own_ref, prev_ref, next_ref,
                kvt, kcat, acc, s_ref, dp_ref, e_ref, ds_ref):
    f32=jnp.float32; bf=jnp.bfloat16
    T=q_ref.shape[2]; count=q_ref.shape[0]; span=2*R+1; W=count+2*R
    for w in range(W):
        if w<R: kw,vw=hp_ref[0,w],hp_ref[1,w]
        elif w<R+count: kw,vw=k_ref[w-R],v_ref[w-R]
        else: kw,vw=hn_ref[0,w-R-count],hn_ref[1,w-R-count]
        kvt[w*T:(w+1)*T,:]=jnp.concatenate([kw,vw],axis=0).T
        kcat[:,w*T:(w+1)*T]=kw
    lane=lax.broadcasted_iota(jnp.int32,(T,2*DH),1)
    zero=jnp.zeros((DH,T),bf)
    for i in range(count):
        q=q_ref[i]*jnp.asarray(0.125,bf); g=g_ref[i]
        q0=jnp.concatenate([q,zero],axis=0); g0=jnp.concatenate([zero,g],axis=0)
        top=None; seen=[]
        for o in range(span):
            w=i+o
            s=jnp.dot(kvt[w*T:(w+1)*T,:],q0,preferred_element_type=f32)
            s_ref[o*T:(o+1)*T,:]=s
            bm=jnp.max(s.reshape(T//8,8,T),axis=0)
            on=vis_ref[i,o]>0
            seen.append(on)
            if abs(o-R)>1: bm=jnp.where(on,bm,-jnp.inf)
            top=bm if top is None else jnp.maximum(top,bm)
        m=jnp.max(top,axis=0,keepdims=True)
        l8=jnp.zeros((8,T),f32); r8=jnp.zeros((8,T),f32)
        for o in range(span):
            w=i+o
            dp=jnp.dot(kvt[w*T:(w+1)*T,:],g0,preferred_element_type=f32)
            mo=jnp.where(seen[o],m,jnp.inf) if abs(o-R)>1 else m
            e=jnp.exp(s_ref[o*T:(o+1)*T,:]-mo)
            dp_ref[o*T:(o+1)*T,:]=dp
            s_ref[o*T:(o+1)*T,:]=e
            e_ref[o*T:(o+1)*T,:]=e.astype(bf)
            l8=l8+jnp.sum(e.reshape(T//8,8,T),axis=0)
            r8=r8+jnp.sum((e*dp).reshape(T//8,8,T),axis=0)
        inv=1.0/jnp.sum(l8,axis=0,keepdims=True)
        delta=jnp.sum(r8,axis=0,keepdims=True)*inv
        qg=(jnp.concatenate([q,g],axis=0).astype(f32)*inv).astype(bf).T
        qt=jnp.where(lane<DH,qg,0); gt=jnp.where(lane<DH,0,qg)
        for o in range(span):
            w=i+o
            sl=slice(o*T,(o+1)*T)
            ds=(s_ref[sl,:]*(dp_ref[sl,:]-delta)).astype(bf)
            ds_ref[sl,:]=ds
            part=jnp.dot(ds,qt,preferred_element_type=f32)+jnp.dot(e_ref[sl,:],gt,preferred_element_type=f32)
            aw=slice(w*T,(w+1)*T)
            if o==span-1 or i==0: acc[aw,:]=part
            else: acc[aw,:]+=part
        dq=jnp.dot(kcat[:,i*T:(i+span)*T],ds_ref[...],preferred_element_type=f32)
        dq_ref[i]=(dq*(inv*0.125)).astype(bf)
    for w in range(W):
        t=acc[w*T:(w+1)*T,:].T
        if w<R: prev_ref[0,w]=t[:DH].astype(bf); prev_ref[1,w]=t[DH:].astype(bf)
        elif w<R+count: own_ref[0,w-R]=t[:DH]; own_ref[1,w-R]=t[DH:]
        else: next_ref[0,w-R-count]=t[:DH].astype(bf); next_ref[1,w-R-count]=t[DH:].astype(bf)

def attn(vis,q,g,k,v,hp,hn,first,heads,kernel=attn_kernel):
    count,_,T=q.shape; span=2*R+1; W=count+2*R
    own=pl.BlockSpec((count,DH,T),lambda h:(0,first+h,0))
    halo=pl.BlockSpec((2,R,DH,T),lambda h:(0,0,h,0))
    n=heads*DH
    f32=jnp.float32; bf=jnp.bfloat16
    return pl.pallas_call(kernel,grid=(heads,),
      in_specs=[pl.BlockSpec(memory_space=pltpu.SMEM),own,own,own,own,halo,halo],
      out_specs=[pl.BlockSpec((count,DH,T),lambda h:(0,h,0)),pl.BlockSpec((2,count,DH,T),lambda h:(0,0,h,0)),halo,halo],
      out_shape=[jax.ShapeDtypeStruct((count,n,T),bf),jax.ShapeDtypeStruct((2,count,n,T),f32),
                 jax.ShapeDtypeStruct((2,R,n,T),bf),jax.ShapeDtypeStruct((2,R,n,T),bf)],
      scratch_shapes=[pltpu.VMEM((W*T,2*DH),bf),pltpu.VMEM((DH,W*T),bf),pltpu.VMEM((W*T,2*DH),f32),
        pltpu.VMEM((span*T,T),f32),pltpu.VMEM((span*T,T),f32),pltpu.VMEM((span*T,T),bf),pltpu.VMEM((span*T,T),bf)],
      compiler_params=pltpu.CompilerParams(vmem_limit_bytes=48*2**20),
      cost_estimate=pl.CostEstimate(flops=heads*count*span*5*2*T*T*DH*4,bytes_accessed=heads*1000000,transcendentals=0),
    )(vis,q,g,k,v,hp,hn)


def route(move):
    views, heads = lax.axis_size("view"), lax.axis_size("head")
    pairs = []
    for g in range(views):
        for h in range(heads):
            to_g, to_h = move(g, h)
            pairs.append((g * heads + h, to_g % views * heads + to_h))
    return pairs


def send(array, move):
    return lax.ppermute(array, ("view", "head"), route(move))


def after(array, *others):
    return lax.optimization_barrier((array, *others))[0]


def local(queries, keys, values, out_grad, out_weight, visible):
    half = jnp.bfloat16
    single = jnp.float32
    count, width, tokens = queries.shape
    me = lax.axis_index("head")
    beside = send(out_grad, lambda g, h: (g, h ^ 2))

    def halos(first, heads, *wait):
        rows = slice(first * DH, (first + heads) * DH)
        last = jnp.stack((keys[count - R :, rows], values[count - R :, rows]))
        initial = jnp.stack((keys[:R, rows], values[:R, rows]))
        if wait:
            last, initial = lax.optimization_barrier((last, initial, *wait))[:2]
        return send(last, lambda g, h: (g + 1, h)), send(initial, lambda g, h: (g - 1, h))

    spans = []
    for heads in CHUNKS:
        spans.append((sum(n for _, n in spans), heads))
    rims = [halos(*spans[0])]
    other = send(jnp.stack((out_grad, beside)), lambda g, h: (g, h ^ 1))
    rims += [halos(*part, beside) for part in spans[1:]]
    order = [me, me ^ 2, me ^ 1, me ^ 3]
    weight = jnp.concatenate(
        [lax.dynamic_slice_in_dim(out_weight, source * width, width, 1) for source in order], 1
    )
    gathered = jnp.concatenate((out_grad, beside, other[0], other[1]), 1)
    attn_grad = jnp.einsum(
        "ij,vjt->vit", weight, gathered, preferred_element_type=single
    ).astype(half)
    query_grads, owned = [], []
    for (first, heads), (before, behind) in zip(spans, rims):
        dq, own, prev, nxt = attn(
            visible, queries, attn_grad, keys, values, before, behind, first, heads
        )
        query_grads.append(dq)
        from_right = send(prev, lambda g, h: (g - 1, h))
        from_left = send(nxt, lambda g, h: (g + 1, h))
        owned.append((own, from_left, from_right))
    totals = []
    for own, from_left, from_right in owned:
        own = own.at[:, :R].add(from_left.astype(single))
        own = own.at[:, count - R :].add(from_right.astype(single))
        totals.append(own)
    total = jnp.concatenate(totals, 2).astype(half)
    return jnp.concatenate(query_grads, 1), total[0], total[1]


def solution(mesh):
    return jax.shard_map(
        local,
        mesh=mesh,
        in_specs=(
            P("view", "head", None),
            P("view", "head", None),
            P("view", "head", None),
            P("view", "head", None),
            P("head", None),
            P("view", None),
        ),
        out_specs=(P("view", "head", None), P("view", "head", None), P("view", "head", None)),
        check_vma=False,
    )
```

```python
import jax
import jax.numpy as jnp
from jax import lax
from jax.experimental import pallas as pl
from jax.experimental.pallas import tpu as pltpu
from jax.sharding import PartitionSpec as P

DH = 64
R = 3
STRIP = 64
GROUPS = ((2, False), (3, False))
PARTS = ((2, False), (2, False), (1, False))


def attn_kernel(
    vis_ref, col_ref, q_ref, g_ref, k_ref, v_ref, near_ref, far_ref, *rest
):
    (
        dq_ref, own_ref, near_out, far_out,
        kvt, kcat, acc, s_ref, dp_ref, pe_ref,
    ) = rest[-10:]
    single = jnp.float32
    half = jnp.bfloat16
    count, _, T = q_ref.shape
    span = 2 * R + 1
    first = col_ref[0] == 0
    skip = col_ref[0] if near_ref.shape[1] > R else 0

    def window(w):
        if w < R:
            return [jnp.where(first, far_ref[n, w], near_ref[n, skip + w]) for n in (0, 1)]
        if w < R + count:
            return k_ref[w - R], v_ref[w - R]
        w -= R + count
        return [jnp.where(first, near_ref[n, skip + w], far_ref[n, w]) for n in (0, 1)]

    for w in range(count + 2 * R):
        key, value = window(w)
        rows = slice(w * T, (w + 1) * T)
        kvt[rows, :] = jnp.concatenate([key, value], axis=0).T
        kcat[:, rows] = key
    lane = lax.broadcasted_iota(jnp.int32, (T, 2 * DH), 1)
    zero = jnp.zeros((DH, T), half)
    state = {}

    def fold(x, op):
        return op(x.reshape(x.shape[0] // 8, 8, T), axis=0)

    def begin(i):
        q = q_ref[i] * jnp.asarray(DH**-0.5, half)
        g = g_ref[i]
        state[i] = dict(
            q=q, g=g, q0=jnp.concatenate([q, zero], axis=0),
            g0=jnp.concatenate([zero, g], axis=0), top=None,
            total=jnp.zeros((8, T), single), cross=jnp.zeros((8, T), single))

    def score(i, o):
        z, w, b = state[i], i + o, i % 2
        s = jnp.dot(kvt[w * T : (w + 1) * T, :], z["q0"], preferred_element_type=single)
        s_ref[b, o * T : (o + 1) * T, :] = s
        best = fold(s, jnp.max)
        if abs(o - R) > 1:
            best = jnp.where(vis_ref[i, o] > 0, best, -jnp.inf)
        z["top"] = best if z["top"] is None else jnp.maximum(z["top"], best)

    def weigh(i, o):
        z, w, b = state[i], i + o, i % 2
        if o == 0:
            z["top"] = jnp.max(z["top"], axis=0, keepdims=True)
        top = z["top"]
        floor = jnp.where(vis_ref[i, o] > 0, top, jnp.inf) if abs(o - R) > 1 else top
        dp = jnp.dot(kvt[w * T : (w + 1) * T, :], z["g0"], preferred_element_type=single)
        for c in range(0, T, STRIP):
            rows = slice(o * T + c, o * T + c + STRIP)
            e = jnp.exp(s_ref[b, rows, :] - floor)
            z["total"] += fold(e, jnp.sum)
            pe_ref[b, rows, T:] = e.astype(half)
            d = dp[c : c + STRIP]
            z["cross"] += fold(e * d, jnp.sum)
            dp_ref[b, rows, :] = d.astype(dp_ref.dtype)

    def norm(i):
        z = state[i]
        z["inv"] = inv = 1.0 / jnp.sum(z["total"], axis=0, keepdims=True)
        z["delta"] = jnp.sum(z["cross"], axis=0, keepdims=True) * inv
        qg = (jnp.concatenate([z["q"], z["g"]], axis=0).astype(single) * inv).astype(half).T
        z["qgt"] = jnp.concatenate([jnp.where(lane < DH, qg, 0), jnp.where(lane < DH, 0, qg)], axis=0)
        z["dq"] = None

    def spread(i, o):
        z, w, b = state[i], i + o, i % 2
        for c in range(0, T, STRIP):
            rows = slice(o * T + c, o * T + c + STRIP)
            ds = pe_ref[b, rows, T:].astype(single) * (dp_ref[b, rows, :].astype(single) - z["delta"])
            pe_ref[b, rows, :T] = ds.astype(half)
        rows = slice(o * T, (o + 1) * T)
        part = jnp.dot(pe_ref[b, rows, :], z["qgt"], preferred_element_type=single)
        there = slice(w * T, (w + 1) * T)
        if o == span - 1 or i == 0:
            acc[there, :] = part
        else:
            acc[there, :] += part
        dq = jnp.dot(kcat[:, there], pe_ref[b, rows, :T], preferred_element_type=single)
        z["dq"] = dq if z["dq"] is None else z["dq"] + dq

    def finish(i):
        z = state[i]
        dq_ref[i] = (z["dq"] * (z["inv"] * DH**-0.5)).astype(half)

    for step in range(count + 2):
        for at, start in ((step, begin), (step - 2, norm)):
            if 0 <= at < count:
                start(at)
        for o in range(span):
            for at, stage in ((step - 2, spread), (step - 1, weigh), (step, score)):
                if 0 <= at < count:
                    stage(at, o)
        if step >= 2:
            finish(step - 2)

    def taken(w):
        return acc[w * T : (w + 1) * T, :].T

    for w in range(count):
        both = taken(R + w)
        own_ref[0, w], own_ref[1, w] = both[:DH], both[DH:]
    for w in range(R):
        low, high = taken(w), taken(R + count + w)
        for ref, both in (
            (near_out, jnp.where(first, high, low).astype(half)),
            (far_out, jnp.where(first, low, high).astype(half)),
        ):
            ref[0, w], ref[1, w] = both[:DH], both[DH:]


def attn(visible, column, queries, grads, keys, values, near, far, first, skipped, heads, so_far):
    count, _, T = queries.shape
    span = 2 * R + 1
    windows = (count + 2 * R) * T
    single = jnp.float32
    half = jnp.bfloat16

    def block(*lead, at=0):
        zeros = (0,) * len(lead)
        return pl.BlockSpec((*lead, DH, T), lambda h: (*zeros, at + h, 0))

    own = block(count, at=first)
    smem = pl.BlockSpec(memory_space=pltpu.SMEM)
    width = heads * DH
    return pl.pallas_call(
        attn_kernel,
        grid=(heads,),
        in_specs=[smem, smem, own, own, own, own, block(2, near.shape[1], at=skipped), block(2, R, at=skipped)]
        + [pl.BlockSpec(memory_space=pl.ANY)] * len(so_far),
        out_specs=[own, block(2, count, at=first), block(2, R), block(2, R)],
        out_shape=[
            jax.ShapeDtypeStruct(queries.shape, half),
            jax.ShapeDtypeStruct((2, *queries.shape), single),
            jax.ShapeDtypeStruct((2, R, width, T), half),
            jax.ShapeDtypeStruct((2, R, width, T), half),
        ],
        scratch_shapes=[
            pltpu.VMEM((windows, 2 * DH), half),
            pltpu.VMEM((DH, windows), half),
            pltpu.VMEM((windows, 2 * DH), single),
            pltpu.VMEM((2, span * T, T), single),
            pltpu.VMEM((2, span * T, T), half),
            pltpu.VMEM((2, span * T, 2 * T), half),
        ],
        input_output_aliases={8 + n: n for n in range(len(so_far))},
        compiler_params=pltpu.CompilerParams(vmem_limit_bytes=40 * 2**20),
        cost_estimate=pl.CostEstimate(
            flops=heads * count * span * 40 * T * T * DH,
            bytes_accessed=heads * 4 * 2**20,
            transcendentals=heads * count * span * T * T,
        ),
    )(visible, column, queries, grads, keys, values, near, far, *so_far)

def send(array, move, label):
    views, heads = lax.axis_size("view"), lax.axis_size("head")
    pairs = []
    for g in range(views):
        for h in range(heads):
            to_g, to_h = move(g, h)
            pairs.append((g * heads + h, to_g % views * heads + to_h))
    with jax.named_scope(label):
        return lax.ppermute(array, ("view", "head"), pairs)


def to_near(g, h):
    return g ^ 1, h


def to_far(g, h):
    return (g - 1, h) if g % 2 == 0 else (g + 1, h)


def along(g, h):
    return (g + 2, h) if g % 2 == 0 else (g - 2, h)


def against(g, h):
    return (g - 2, h) if g % 2 == 0 else (g + 2, h)


def local(queries, keys, values, out_grad, out_weight, visible):
    half = jnp.bfloat16
    single = jnp.float32
    count, width, tokens = queries.shape
    me = lax.axis_index("head")
    column = lax.axis_index("view") % 2

    def views(array, at):
        return lax.dynamic_slice_in_dim(array, at, R, 1)

    def spans(parts):
        start = 0
        for heads, shared in parts:
            yield start, heads, shared
            start += heads

    def halos(first, heads, shared, wait):
        rows = slice(first * DH, (first + heads) * DH)
        pair = jnp.stack((keys[:, rows], values[:, rows]))
        if wait is not None:
            pair = lax.optimization_barrier((pair, wait))[0]
        if shared:
            near = send(pair, to_near, f"in_near_{first}")
            far = send(views(near, 1 - column), along, f"in_far_{first}")
        else:
            near = send(views(pair, 1 - column), to_near, f"in_near_{first}")
            far = send(views(pair, column), to_far, f"in_far_{first}")
        return near, far

    beside = send(out_grad, lambda g, h: (g, h ^ 2), "beside")
    groups = list(spans(GROUPS))
    rims = [halos(*groups[0], None)]
    twin = send(out_grad, lambda g, h: (g, h ^ 1), "twin")
    across = send(beside, lambda g, h: (g, h ^ 1), "across")
    for part in groups[1:]:
        rims.append(halos(*part, beside))
    order = [me, me ^ 1, me ^ 2, me ^ 3]
    weight = jnp.concatenate(
        [lax.dynamic_slice_in_dim(out_weight, source * width, width, 1) for source in order], 1
    )
    gathered = jnp.concatenate((out_grad, twin, beside, across), 1)
    attn_grad = jnp.einsum(
        "ij,vjt->vit", weight, gathered, preferred_element_type=single
    ).astype(half)
    so_far, backs = (), []
    for first, heads, shared in spans(PARTS):
        group = max(n for n, (start, _, _) in enumerate(groups) if start <= first)
        near, far = rims[group]
        if len(backs) > 1:
            near, *backs[-2] = lax.optimization_barrier((near, *backs[-2]))
        query_grads, own, near_part, far_part = attn(
            visible, column[None], queries, attn_grad, keys, values, near, far, first,
            first - groups[group][0], heads, so_far,
        )
        so_far = (query_grads, own)
        if first == 0:
            near_part, far_part, *rims[1] = lax.optimization_barrier(
                (near_part, far_part, *rims[1])
            )
        if shared:
            back = send(far_part, against, f"out_far_{first}")
            both = jnp.zeros((2, count, *near_part.shape[2:]), single)
            place = lambda part, at: lax.dynamic_update_slice_in_dim(
                both, part.astype(single), at, 1
            )
            both = (place(near_part, column) + place(back, 1 - column)).astype(half)
            backs.append([send(both, to_near, f"out_near_{first}")])
        else:
            backs.append([send(near_part, to_near, f"out_near_{first}"), send(far_part, to_far, f"out_far_{first}")])
    tail = lax.optimization_barrier((*backs[-2], *backs[-1]))
    backs[-2:] = [tail[: len(backs[-2])], tail[len(backs[-2]) :]]
    sums = []
    for (first, heads, _), (near, *far) in zip(spans(PARTS), backs):
        mine = own[:, :, first * DH : (first + heads) * DH]
        if not far:
            mine = mine + near.astype(single)
        else:
            low = jnp.where(column == 0, far[0], near).astype(single)
            high = jnp.where(column == 0, near, far[0]).astype(single)
            mine = mine.at[:, :R].add(low).at[:, count - R :].add(high)
        sums.append(mine.astype(half))
    total = jnp.concatenate(sums, 2)
    return query_grads, total[0], total[1]


def solution(mesh):
    return jax.shard_map(
        local,
        mesh=mesh,
        in_specs=(
            P("view", "head", None),
            P("view", "head", None),
            P("view", "head", None),
            P("view", "head", None),
            P("head", None),
            P("view", None),
        ),
        out_specs=(P("view", "head", None), P("view", "head", None), P("view", "head", None)),
        check_vma=False,
    )
```

```python
import jax
import jax.numpy as jnp
from jax import lax
from jax.experimental import pallas as pl
from jax.experimental.pallas import tpu as pltpu
from jax.sharding import PartitionSpec as P

DH = 64
R = 3
STRIP = 64
GROUPS = ((2, True), (2, False), (1, False))
PARTS = ((2, False), (2, False), (1, False))


def attn_kernel(
    vis_ref, col_ref, q_ref, g_ref, k_ref, v_ref, near_ref, far_ref, *rest
):
    (
        dq_ref, own_ref, near_out, far_out,
        kvt, kcat, acc, s_ref, dp_ref, pe_ref,
    ) = rest[-10:]
    single = jnp.float32
    half = jnp.bfloat16
    count, _, T = q_ref.shape
    span = 2 * R + 1
    first = col_ref[0] == 0
    skip = col_ref[0] if near_ref.shape[1] > R else 0

    def window(w):
        if w < R:
            return [jnp.where(first, far_ref[n, w], near_ref[n, skip + w]) for n in (0, 1)]
        if w < R + count:
            return k_ref[w - R], v_ref[w - R]
        w -= R + count
        return [jnp.where(first, near_ref[n, skip + w], far_ref[n, w]) for n in (0, 1)]

    for w in range(count + 2 * R):
        key, value = window(w)
        rows = slice(w * T, (w + 1) * T)
        kvt[rows, :] = jnp.concatenate([key, value], axis=0).T
        kcat[:, rows] = key
    lane = lax.broadcasted_iota(jnp.int32, (T, 2 * DH), 1)
    zero = jnp.zeros((DH, T), half)
    state = {}

    def fold(x, op):
        return op(x.reshape(x.shape[0] // 8, 8, T), axis=0)

    def begin(i):
        q = q_ref[i] * jnp.asarray(DH**-0.5, half)
        g = g_ref[i]
        state[i] = dict(
            q=q, g=g, q0=jnp.concatenate([q, zero], axis=0),
            g0=jnp.concatenate([zero, g], axis=0), top=None,
            total=jnp.zeros((8, T), single), cross=jnp.zeros((8, T), single))

    def score(i, o):
        z, w, b = state[i], i + o, i % 2
        s = jnp.dot(kvt[w * T : (w + 1) * T, :], z["q0"], preferred_element_type=single)
        s_ref[b, o * T : (o + 1) * T, :] = s
        best = fold(s, jnp.max)
        if abs(o - R) > 1:
            best = jnp.where(vis_ref[i, o] > 0, best, -jnp.inf)
        z["top"] = best if z["top"] is None else jnp.maximum(z["top"], best)

    def weigh(i, o):
        z, w, b = state[i], i + o, i % 2
        if o == 0:
            z["top"] = jnp.max(z["top"], axis=0, keepdims=True)
        top = z["top"]
        floor = jnp.where(vis_ref[i, o] > 0, top, jnp.inf) if abs(o - R) > 1 else top
        dp = jnp.dot(kvt[w * T : (w + 1) * T, :], z["g0"], preferred_element_type=single)
        for c in range(0, T, STRIP):
            rows = slice(o * T + c, o * T + c + STRIP)
            e = jnp.exp(s_ref[b, rows, :] - floor)
            z["total"] += fold(e, jnp.sum)
            pe_ref[b, rows, T:] = e.astype(half)
            d = dp[c : c + STRIP]
            z["cross"] += fold(e * d, jnp.sum)
            dp_ref[b, rows, :] = d.astype(dp_ref.dtype)

    def norm(i):
        z = state[i]
        z["inv"] = inv = 1.0 / jnp.sum(z["total"], axis=0, keepdims=True)
        z["delta"] = jnp.sum(z["cross"], axis=0, keepdims=True) * inv
        qg = (jnp.concatenate([z["q"], z["g"]], axis=0).astype(single) * inv).astype(half).T
        z["qgt"] = jnp.concatenate([jnp.where(lane < DH, qg, 0), jnp.where(lane < DH, 0, qg)], axis=0)
        z["dq"] = None

    def spread(i, o):
        z, w, b = state[i], i + o, i % 2
        for c in range(0, T, STRIP):
            rows = slice(o * T + c, o * T + c + STRIP)
            ds = pe_ref[b, rows, T:].astype(single) * (dp_ref[b, rows, :].astype(single) - z["delta"])
            pe_ref[b, rows, :T] = ds.astype(half)
        rows = slice(o * T, (o + 1) * T)
        part = jnp.dot(pe_ref[b, rows, :], z["qgt"], preferred_element_type=single)
        there = slice(w * T, (w + 1) * T)
        if o == span - 1 or i == 0:
            acc[there, :] = part
        else:
            acc[there, :] += part
        dq = jnp.dot(kcat[:, there], pe_ref[b, rows, :T], preferred_element_type=single)
        z["dq"] = dq if z["dq"] is None else z["dq"] + dq

    def finish(i):
        z = state[i]
        dq_ref[i] = (z["dq"] * (z["inv"] * DH**-0.5)).astype(half)

    for step in range(count + 2):
        for at, start in ((step, begin), (step - 2, norm)):
            if 0 <= at < count:
                start(at)
        for o in range(span):
            for at, stage in ((step - 2, spread), (step - 1, weigh), (step, score)):
                if 0 <= at < count:
                    stage(at, o)
        if step >= 2:
            finish(step - 2)

    def taken(w):
        return acc[w * T : (w + 1) * T, :].T

    for w in range(count):
        both = taken(R + w)
        own_ref[0, w], own_ref[1, w] = both[:DH], both[DH:]
    for w in range(R):
        low, high = taken(w), taken(R + count + w)
        for ref, both in (
            (near_out, jnp.where(first, high, low).astype(half)),
            (far_out, jnp.where(first, low, high).astype(half)),
        ):
            ref[0, w], ref[1, w] = both[:DH], both[DH:]


def attn(visible, column, queries, grads, keys, values, near, far, first, skipped, heads, so_far):
    count, _, T = queries.shape
    span = 2 * R + 1
    windows = (count + 2 * R) * T
    single = jnp.float32
    half = jnp.bfloat16

    def block(*lead, at=0):
        zeros = (0,) * len(lead)
        return pl.BlockSpec((*lead, DH, T), lambda h: (*zeros, at + h, 0))

    own = block(count, at=first)
    smem = pl.BlockSpec(memory_space=pltpu.SMEM)
    width = heads * DH
    return pl.pallas_call(
        attn_kernel,
        grid=(heads,),
        in_specs=[smem, smem, own, own, own, own, block(2, near.shape[1], at=skipped), block(2, R, at=skipped)]
        + [pl.BlockSpec(memory_space=pl.ANY)] * len(so_far),
        out_specs=[own, block(2, count, at=first), block(2, R), block(2, R)],
        out_shape=[
            jax.ShapeDtypeStruct(queries.shape, half),
            jax.ShapeDtypeStruct((2, *queries.shape), single),
            jax.ShapeDtypeStruct((2, R, width, T), half),
            jax.ShapeDtypeStruct((2, R, width, T), half),
        ],
        scratch_shapes=[
            pltpu.VMEM((windows, 2 * DH), half),
            pltpu.VMEM((DH, windows), half),
            pltpu.VMEM((windows, 2 * DH), single),
            pltpu.VMEM((2, span * T, T), single),
            pltpu.VMEM((2, span * T, T), half),
            pltpu.VMEM((2, span * T, 2 * T), half),
        ],
        input_output_aliases={8 + n: n for n in range(len(so_far))},
        compiler_params=pltpu.CompilerParams(vmem_limit_bytes=40 * 2**20),
        cost_estimate=pl.CostEstimate(
            flops=heads * count * span * 40 * T * T * DH,
            bytes_accessed=heads * 4 * 2**20,
            transcendentals=heads * count * span * T * T,
        ),
    )(visible, column, queries, grads, keys, values, near, far, *so_far)

def send(array, move, label):
    views, heads = lax.axis_size("view"), lax.axis_size("head")
    pairs = []
    for g in range(views):
        for h in range(heads):
            to_g, to_h = move(g, h)
            pairs.append((g * heads + h, to_g % views * heads + to_h))
    with jax.named_scope(label):
        return lax.ppermute(array, ("view", "head"), pairs)


def to_near(g, h):
    return g ^ 1, h


def to_far(g, h):
    return (g - 1, h) if g % 2 == 0 else (g + 1, h)


def along(g, h):
    return (g + 2, h) if g % 2 == 0 else (g - 2, h)


def against(g, h):
    return (g - 2, h) if g % 2 == 0 else (g + 2, h)


def local(queries, keys, values, out_grad, out_weight, visible):
    half = jnp.bfloat16
    single = jnp.float32
    count, width, tokens = queries.shape
    me = lax.axis_index("head")
    column = lax.axis_index("view") % 2

    def views(array, at):
        return lax.dynamic_slice_in_dim(array, at, R, 1)

    def spans(parts):
        start = 0
        for heads, shared in parts:
            yield start, heads, shared
            start += heads

    def halos(first, heads, shared, wait):
        rows = slice(first * DH, (first + heads) * DH)
        pair = jnp.stack((keys[:, rows], values[:, rows]))
        if wait is not None:
            pair = lax.optimization_barrier((pair, wait))[0]
        if shared:
            near = send(pair, to_near, f"in_near_{first}")
            far = send(views(near, 1 - column), along, f"in_far_{first}")
        else:
            near = send(views(pair, 1 - column), to_near, f"in_near_{first}")
            far = send(views(pair, column), to_far, f"in_far_{first}")
        return near, far

    beside = send(out_grad, lambda g, h: (g, h ^ 2), "beside")
    groups = list(spans(GROUPS))
    rims = [halos(*groups[0], None)]
    twin = send(out_grad, lambda g, h: (g, h ^ 1), "twin")
    across = send(beside, lambda g, h: (g, h ^ 1), "across")
    for part in groups[1:]:
        rims.append(halos(*part, beside))
    order = [me, me ^ 1, me ^ 2, me ^ 3]
    weight = jnp.concatenate(
        [lax.dynamic_slice_in_dim(out_weight, source * width, width, 1) for source in order], 1
    )
    gathered = jnp.concatenate((out_grad, twin, beside, across), 1)
    attn_grad = jnp.einsum(
        "ij,vjt->vit", weight, gathered, preferred_element_type=single
    ).astype(half)
    so_far, backs = (), []
    for first, heads, shared in spans(PARTS):
        group = max(n for n, (start, _, _) in enumerate(groups) if start <= first)
        near, far = rims[group]
        if len(backs) > 1:
            near, *backs[-2] = lax.optimization_barrier((near, *backs[-2]))
        query_grads, own, near_part, far_part = attn(
            visible, column[None], queries, attn_grad, keys, values, near, far, first,
            first - groups[group][0], heads, so_far,
        )
        so_far = (query_grads, own)
        if first == 0:
            near_part, far_part, *rims[1] = lax.optimization_barrier(
                (near_part, far_part, *rims[1])
            )
        if shared:
            back = send(far_part, against, f"out_far_{first}")
            both = jnp.zeros((2, count, *near_part.shape[2:]), single)
            place = lambda part, at: lax.dynamic_update_slice_in_dim(
                both, part.astype(single), at, 1
            )
            both = (place(near_part, column) + place(back, 1 - column)).astype(half)
            backs.append([send(both, to_near, f"out_near_{first}")])
        else:
            backs.append([send(near_part, to_near, f"out_near_{first}"), send(far_part, to_far, f"out_far_{first}")])
    tail = lax.optimization_barrier((*backs[-2], *backs[-1]))
    backs[-2:] = [tail[: len(backs[-2])], tail[len(backs[-2]) :]]
    sums = []
    for (first, heads, _), (near, *far) in zip(spans(PARTS), backs):
        mine = own[:, :, first * DH : (first + heads) * DH]
        if not far:
            mine = mine + near.astype(single)
        else:
            low = jnp.where(column == 0, far[0], near).astype(single)
            high = jnp.where(column == 0, near, far[0]).astype(single)
            mine = mine.at[:, :R].add(low).at[:, count - R :].add(high)
        sums.append(mine.astype(half))
    total = jnp.concatenate(sums, 2)
    return query_grads, total[0], total[1]


def solution(mesh):
    return jax.shard_map(
        local,
        mesh=mesh,
        in_specs=(
            P("view", "head", None),
            P("view", "head", None),
            P("view", "head", None),
            P("view", "head", None),
            P("head", None),
            P("view", None),
        ),
        out_specs=(P("view", "head", None), P("view", "head", None), P("view", "head", None)),
        check_vma=False,
    )
```

```python
import jax
import jax.numpy as jnp
from jax import lax
from jax.experimental import pallas as pl
from jax.experimental.pallas import tpu as pltpu
from jax.sharding import PartitionSpec as P

DH = 64
R = 3
STRIP = 16
GROUPS = ((2, True), (2, False), (1, False))
PARTS = ((2, False), (2, False), (1, False))


def attn_kernel(
    vis_ref, col_ref, q_ref, g_ref, k_ref, v_ref, near_ref, far_ref, *rest
):
    (
        dq_ref, own_ref, near_out, far_out,
        kvt, kcat, acc, s_ref, dp_ref, pe_ref,
    ) = rest[-10:]
    single = jnp.float32
    half = jnp.bfloat16
    count, _, T = q_ref.shape
    span = 2 * R + 1
    first = col_ref[0] == 0
    skip = col_ref[0] if near_ref.shape[1] > R else 0

    def window(w):
        if w < R:
            return [jnp.where(first, far_ref[n, w], near_ref[n, skip + w]) for n in (0, 1)]
        if w < R + count:
            return k_ref[w - R], v_ref[w - R]
        w -= R + count
        return [jnp.where(first, near_ref[n, skip + w], far_ref[n, w]) for n in (0, 1)]

    for w in range(count + 2 * R):
        key, value = window(w)
        rows = slice(w * T, (w + 1) * T)
        kvt[rows, :] = jnp.concatenate([key, value], axis=0).T
        kcat[:, rows] = key
    lane = lax.broadcasted_iota(jnp.int32, (T, 2 * DH), 1)
    zero = jnp.zeros((DH, T), half)
    state = {}

    def fold(x, op):
        return op(x.reshape(x.shape[0] // 8, 8, T), axis=0)

    def begin(i):
        q = q_ref[i] * jnp.asarray(DH**-0.5, half)
        g = g_ref[i]
        state[i] = dict(
            q=q, g=g, q0=jnp.concatenate([q, zero], axis=0),
            g0=jnp.concatenate([zero, g], axis=0), top=None,
            total=jnp.zeros((8, T), single), cross=jnp.zeros((8, T), single))

    def score(i, o):
        z, w, b = state[i], i + o, i % 2
        s = jnp.dot(kvt[w * T : (w + 1) * T, :], z["q0"], preferred_element_type=single)
        s_ref[b, o * T : (o + 1) * T, :] = s
        best = fold(s, jnp.max)
        if abs(o - R) > 1:
            best = jnp.where(vis_ref[i, o] > 0, best, -jnp.inf)
        z["top"] = best if z["top"] is None else jnp.maximum(z["top"], best)

    def weigh(i, o):
        z, w, b = state[i], i + o, i % 2
        if o == 0:
            z["top"] = jnp.max(z["top"], axis=0, keepdims=True)
        top = z["top"]
        floor = jnp.where(vis_ref[i, o] > 0, top, jnp.inf) if abs(o - R) > 1 else top
        dp = jnp.dot(kvt[w * T : (w + 1) * T, :], z["g0"], preferred_element_type=single)
        for c in range(0, T, STRIP):
            rows = slice(o * T + c, o * T + c + STRIP)
            e = jnp.exp(s_ref[b, rows, :] - floor)
            z["total"] += fold(e, jnp.sum)
            pe_ref[b, rows, T:] = e.astype(half)
            d = dp[c : c + STRIP]
            z["cross"] += fold(e * d, jnp.sum)
            dp_ref[b, rows, :] = d.astype(dp_ref.dtype)

    def norm(i):
        z = state[i]
        z["inv"] = inv = 1.0 / jnp.sum(z["total"], axis=0, keepdims=True)
        z["delta"] = jnp.sum(z["cross"], axis=0, keepdims=True) * inv
        qg = (jnp.concatenate([z["q"], z["g"]], axis=0).astype(single) * inv).astype(half).T
        z["qgt"] = jnp.concatenate([jnp.where(lane < DH, qg, 0), jnp.where(lane < DH, 0, qg)], axis=0)
        z["dq"] = None

    def spread(i, o):
        z, w, b = state[i], i + o, i % 2
        for c in range(0, T, STRIP):
            rows = slice(o * T + c, o * T + c + STRIP)
            ds = pe_ref[b, rows, T:].astype(single) * (dp_ref[b, rows, :].astype(single) - z["delta"])
            pe_ref[b, rows, :T] = ds.astype(half)
        rows = slice(o * T, (o + 1) * T)
        part = jnp.dot(pe_ref[b, rows, :], z["qgt"], preferred_element_type=single)
        there = slice(w * T, (w + 1) * T)
        if o == span - 1 or i == 0:
            acc[there, :] = part
        else:
            acc[there, :] += part
        dq = jnp.dot(kcat[:, there], pe_ref[b, rows, :T], preferred_element_type=single)
        z["dq"] = dq if z["dq"] is None else z["dq"] + dq

    def finish(i):
        z = state[i]
        dq_ref[i] = (z["dq"] * (z["inv"] * DH**-0.5)).astype(half)

    for step in range(count + 2):
        for at, start in ((step, begin), (step - 2, norm)):
            if 0 <= at < count:
                start(at)
        for o in range(span):
            for at, stage in ((step - 2, spread), (step - 1, weigh), (step, score)):
                if 0 <= at < count:
                    stage(at, o)
        if step >= 2:
            finish(step - 2)

    def taken(w):
        return acc[w * T : (w + 1) * T, :].T

    for w in range(count):
        both = taken(R + w)
        own_ref[0, w], own_ref[1, w] = both[:DH].astype(half), both[DH:].astype(half)
    for w in range(R):
        low, high = taken(w), taken(R + count + w)
        for ref, both in (
            (near_out, jnp.where(first, high, low).astype(half)),
            (far_out, jnp.where(first, low, high).astype(half)),
        ):
            ref[0, w], ref[1, w] = both[:DH], both[DH:]


def attn(visible, column, queries, grads, keys, values, near, far, first, skipped, heads, so_far):
    count, _, T = queries.shape
    span = 2 * R + 1
    windows = (count + 2 * R) * T
    single = jnp.float32
    half = jnp.bfloat16

    def block(*lead, at=0):
        zeros = (0,) * len(lead)
        return pl.BlockSpec((*lead, DH, T), lambda h: (*zeros, at + h, 0))

    own = block(count, at=first)
    smem = pl.BlockSpec(memory_space=pltpu.SMEM)
    width = heads * DH
    return pl.pallas_call(
        attn_kernel,
        grid=(heads,),
        in_specs=[smem, smem, own, own, own, own, block(2, near.shape[1], at=skipped), block(2, R, at=skipped)]
        + [pl.BlockSpec(memory_space=pl.ANY)] * len(so_far),
        out_specs=[own, block(2, count, at=first), block(2, R), block(2, R)],
        out_shape=[
            jax.ShapeDtypeStruct(queries.shape, half),
            jax.ShapeDtypeStruct((2, *queries.shape), half),
            jax.ShapeDtypeStruct((2, R, width, T), half),
            jax.ShapeDtypeStruct((2, R, width, T), half),
        ],
        scratch_shapes=[
            pltpu.VMEM((windows, 2 * DH), half),
            pltpu.VMEM((DH, windows), half),
            pltpu.VMEM((windows, 2 * DH), single),
            pltpu.VMEM((2, span * T, T), single),
            pltpu.VMEM((2, span * T, T), half),
            pltpu.VMEM((2, span * T, 2 * T), half),
        ],
        input_output_aliases={8 + n: n for n in range(len(so_far))},
        compiler_params=pltpu.CompilerParams(vmem_limit_bytes=40 * 2**20),
        cost_estimate=pl.CostEstimate(
            flops=heads * count * span * 40 * T * T * DH,
            bytes_accessed=heads * 4 * 2**20,
            transcendentals=heads * count * span * T * T,
        ),
    )(visible, column, queries, grads, keys, values, near, far, *so_far)

def send(array, move, label):
    views, heads = lax.axis_size("view"), lax.axis_size("head")
    pairs = []
    for g in range(views):
        for h in range(heads):
            to_g, to_h = move(g, h)
            pairs.append((g * heads + h, to_g % views * heads + to_h))
    with jax.named_scope(label):
        return lax.ppermute(array, ("view", "head"), pairs)


def to_near(g, h):
    return g ^ 1, h


def to_far(g, h):
    return (g - 1, h) if g % 2 == 0 else (g + 1, h)


def along(g, h):
    return (g + 2, h) if g % 2 == 0 else (g - 2, h)


def against(g, h):
    return (g - 2, h) if g % 2 == 0 else (g + 2, h)


def local(queries, keys, values, out_grad, out_weight, visible):
    half = jnp.bfloat16
    single = jnp.float32
    count, width, tokens = queries.shape
    me = lax.axis_index("head")
    column = lax.axis_index("view") % 2

    def views(array, at):
        return lax.dynamic_slice_in_dim(array, at, R, 1)

    def spans(parts):
        start = 0
        for heads, shared in parts:
            yield start, heads, shared
            start += heads

    def halos(first, heads, shared, wait):
        rows = slice(first * DH, (first + heads) * DH)
        pair = jnp.stack((keys[:, rows], values[:, rows]))
        if wait is not None:
            pair = lax.optimization_barrier((pair, wait))[0]
        if shared:
            near = send(pair, to_near, f"in_near_{first}")
            far = send(views(near, 1 - column), along, f"in_far_{first}")
        else:
            near = send(views(pair, 1 - column), to_near, f"in_near_{first}")
            far = send(views(pair, column), to_far, f"in_far_{first}")
        return near, far

    beside = send(out_grad, lambda g, h: (g, h ^ 2), "beside")
    groups = list(spans(GROUPS))
    rims = [halos(*groups[0], None)]
    twin = send(out_grad, lambda g, h: (g, h ^ 1), "twin")
    across = send(beside, lambda g, h: (g, h ^ 1), "across")
    for part in groups[1:]:
        rims.append(halos(*part, beside))
    order = [me, me ^ 1, me ^ 2, me ^ 3]
    weight = jnp.concatenate(
        [lax.dynamic_slice_in_dim(out_weight, source * width, width, 1) for source in order], 1
    )
    gathered = jnp.concatenate((out_grad, twin, beside, across), 1)
    attn_grad = jnp.einsum(
        "ij,vjt->vit", weight, gathered, preferred_element_type=single
    ).astype(half)
    so_far, backs = (), []
    for first, heads, shared in spans(PARTS):
        group = max(n for n, (start, _, _) in enumerate(groups) if start <= first)
        near, far = rims[group]
        if len(backs) > 1:
            near, *backs[-2] = lax.optimization_barrier((near, *backs[-2]))
        query_grads, own, near_part, far_part = attn(
            visible, column[None], queries, attn_grad, keys, values, near, far, first,
            first - groups[group][0], heads, so_far,
        )
        so_far = (query_grads, own)
        if first == 0:
            near_part, far_part, *rims[1] = lax.optimization_barrier(
                (near_part, far_part, *rims[1])
            )
        if shared:
            back = send(far_part, against, f"out_far_{first}")
            both = jnp.zeros((2, count, *near_part.shape[2:]), single)
            place = lambda part, at: lax.dynamic_update_slice_in_dim(
                both, part.astype(single), at, 1
            )
            both = (place(near_part, column) + place(back, 1 - column)).astype(half)
            backs.append([send(both, to_near, f"out_near_{first}")])
        else:
            backs.append([send(near_part, to_near, f"out_near_{first}"), send(far_part, to_far, f"out_far_{first}")])
    tail = lax.optimization_barrier((*backs[-2], *backs[-1]))
    backs[-2:] = [tail[: len(backs[-2])], tail[len(backs[-2]) :]]
    sums = []
    for (first, heads, _), (near, *far) in zip(spans(PARTS), backs):
        mine = own[:, :, first * DH : (first + heads) * DH].astype(single)
        if not far:
            mine = mine + near.astype(single)
        else:
            low = jnp.where(column == 0, far[0], near).astype(single)
            high = jnp.where(column == 0, near, far[0]).astype(single)
            mine = mine.at[:, :R].add(low).at[:, count - R :].add(high)
        sums.append(mine.astype(half))
    total = jnp.concatenate(sums, 2)
    return query_grads, total[0], total[1]


def solution(mesh):
    return jax.shard_map(
        local,
        mesh=mesh,
        in_specs=(
            P("view", "head", None),
            P("view", "head", None),
            P("view", "head", None),
            P("view", "head", None),
            P("head", None),
            P("view", None),
        ),
        out_specs=(P("view", "head", None), P("view", "head", None), P("view", "head", None)),
        check_vma=False,
    )
```
